32 devices in a mesh: gx: 4 (over x, core), yz: 8 (over z, y).
Axes of the slice: x: 2, y: 2, z: 4, core: 2. Of those that a mesh axis runs over, the one named last changes fastest.
Arguments:
- owners: int32 [4096, 1], P(('gx', 'yz')), may hold values from 0 to 31; in each aligned block of 128 rows (0 to 127, 128 to 255, ...) at most 8 rows name the same one
- bricks: int32 [4096], P(('gx', 'yz')), may hold values from 0 to 63
- cells: int32 [4096, 3, 128], P(('gx', 'yz')), may hold values from 0 to 7
- offsets: float32 [4096, 3, 128], P(('gx', 'yz')), may hold values from 0.5 to 1.5
- mass: float32 [4096, 128], P(('gx', 'yz')), may hold values from 0.5 to 2
- velocity: float32 [4096, 3, 128], P(('gx', 'yz')), may hold values from -6 to 6
- affine: float32 [4096, 9, 128], P(('gx', 'yz')), may hold values from -4 to 4
Outputs:
- grid_mass: float32 [64, 128, 128], P('gx', 'yz')
- grid_velocity: float32 [3, 64, 128, 128], P(None, 'gx', 'yz')
The draws below stay inside these ranges and needn't reach their ends.
Inputs may be any that keep to these rules, and one draw needn't show every extreme that they name: In the owners of each aligned group of 128 rows (the blocks of one device) no device is named more than 8 times, and some device is named exactly 8 times.
All inputs are finite; a program needn't handle non-finite values.
Results may differ from the reference program's by a relative error of at most 0.0003.
Values sent between devices are 32-bit elements; how exact they have to be, the bound alone decides.
A program may use at most 128 MiB of HBM per device.

```python
import math
import jax
import jax.numpy as jnp
import numpy as np

PB = 128
BRICK = 8
NB_DEV = 128
FACE = 16
CZ = 128
BRICKS_DEV = 64
CAP = 8
BLOCKS = 4096
N_GX = 4
N_YZ = 8
DEVICES = 32


def with_ends(result, rng, low, largest):
    longest = result.shape.index(max(result.shape))
    spots = []
    for shift in (0, 1):
        where = [jax.random.randint(jax.random.fold_in(rng, axis), (), 0, length) for axis, length in enumerate(result.shape)]
        where[longest] = (where[longest] + shift) % result.shape[longest]
        spots.append(tuple(where))
    return result.at[spots[0]].set(low).at[spots[1]].set(largest)


def steps_of(rng, dims, shards, low, largest):
    gain = 1.0
    for position, blocks in shards:
        steps = jax.random.uniform(jax.random.fold_in(jax.random.fold_in(rng, 6), position), (blocks,), jnp.float32, low / len(shards), largest / len(shards))
        gain = gain * jnp.repeat(jnp.exp(steps), dims[position] // blocks).reshape((-1,) + (1,) * (len(dims) - 1 - position))
    return gain


def routed_block(own_key, own, number, rows, count, top, bound, lean):
    sequence = jax.random.permutation(own_key, count)
    heavy_load, common = portions_of(count, rows * top, bound, lean, True), portions_of(count, rows * top, bound, lean, False)
    places = jnp.arange(count)

    def named(lengths, rotation):
        used = int((lengths > 0).sum())
        fixed = max(1, used // 4)
        moved = fixed + (places - fixed + rotation * (used - fixed)) % max(1, count - fixed)
        return jnp.zeros((count,), jnp.int32).at[sequence[jnp.where(places < fixed, places, moved)]].set(jnp.asarray(lengths, jnp.int32))

    lengths = jnp.where(number % 4 == 0, named(heavy_load, number // 4), named(common, number - number // 4 - 1))
    mixed = jax.random.permutation(jax.random.fold_in(own, 3), count)
    donor, sink = mixed[0:count // 2 * 2:2], mixed[1:count // 2 * 2:2]
    room = jnp.minimum(lengths[donor] - 1, bound - lengths[sink]) // 2
    room = jnp.where((donor == sequence[0]) | (sink == sequence[0]) | (lengths[sink] == 0), 0, jnp.maximum(room, 0))
    moved = jax.random.randint(jax.random.fold_in(own, 4), (count // 2,), 0, 1 << 20) % (room + 1)
    lengths = lengths.at[donor].add(-moved).at[sink].add(moved)
    labels = jnp.searchsorted(jnp.cumsum(lengths), jnp.arange(rows * top), side="right").astype(jnp.int32)
    table = labels.reshape(top, rows).T
    table = table[jax.random.permutation(jax.random.fold_in(own, 1), rows)]
    rotation = jax.random.randint(jax.random.fold_in(own, 2), (rows, 1), 0, top)
    return jnp.take_along_axis(table, (jnp.arange(top)[None, :] + rotation) % top, axis=1)


def portions_of(number_of, total, reach, skew, full):
    loads = [(1 << 20) // math.isqrt(grade ** skew) + 1 for grade in range(1, number_of + 1)]
    largest = reach if full else min(reach, max(-(-total // number_of), total * loads[0] // sum(loads)))
    least = 1 if total - largest >= number_of - 1 else 0
    holding, rest = [largest] + [least] * (number_of - 1), total - largest - least * (number_of - 1)
    while rest > 0:
        free = [i for i in range(1, number_of) if holding[i] < largest] or [i for i in range(1, number_of) if holding[i] < reach]
        whole, remaining = sum([loads[i] for i in free]), rest
        for i in free:
            more = min(reach - holding[i], max(1, remaining * loads[i] // whole), rest)
            holding[i] = holding[i] + more
            rest = rest - more
    return np.array(holding)


def scatter_about(rng, dims, spread, limit, pieces=(), kind=jnp.bfloat16):
    drawn = jax.random.normal(rng, dims, jnp.float32) * spread
    if len(pieces) > 0:
        drawn = steps_of(rng, dims, pieces, -0.22, 0.18) * drawn
    return jnp.clip(drawn, min=-limit, max=limit).astype(kind)


def setup_inputs(seed: int = 0) -> dict:
    splits = jax.random.split(jax.random.key(seed), 8)
    owners_keys = jax.random.split(jax.random.fold_in(splits[0], 1), BLOCKS // NB_DEV)
    owners_turns = jax.random.permutation(jax.random.fold_in(splits[0], 3), BLOCKS // NB_DEV)
    owners = jax.vmap(lambda own, number: routed_block(jax.random.fold_in(splits[0], 2), own, number, NB_DEV, DEVICES, 1, CAP, 2))(owners_keys, owners_turns).reshape((BLOCKS, 1))
    bricks = with_ends(jax.random.randint(splits[1], (BLOCKS,), 0, BRICKS_DEV), jax.random.fold_in(splits[1], 1), 0, BRICKS_DEV - 1).astype(jnp.int32)
    cells = with_ends(jax.random.randint(splits[2], (BLOCKS, 3, PB), 0, BRICK), jax.random.fold_in(splits[2], 1), 0, BRICK - 1).astype(jnp.int32)
    offsets = jnp.clip(0.5 + 1.0 * jax.random.uniform(splits[3], (BLOCKS, 3, PB), jnp.float32) ** steps_of(splits[3], (BLOCKS, 3, PB), ((0, 32),), -0.2, 0.2), 0.5, 1.5)
    mass = jnp.clip(jnp.exp(math.log(2.0) - 1.3862944 * jax.random.uniform(splits[4], (BLOCKS, PB), jnp.float32) ** steps_of(splits[4], (BLOCKS, PB), ((0, 32),), -0.2, 0.2)), 0.5, 2.0)
    velocity = scatter_about(splits[5], (BLOCKS, 3, PB), 1.0, 6.0, ((0, 32),), jnp.float32)
    affine = scatter_about(splits[6], (BLOCKS, 9, PB), 0.5, 4.0, ((0, 32),), jnp.float32)
    return dict(owners=owners, bricks=bricks, cells=cells, offsets=offsets, mass=mass, velocity=velocity, affine=affine)


def spline(frac):
    return (0.5 * (1.5 - frac) ** 2, 0.75 - (frac - 1.0) ** 2, 0.5 * (frac - 0.5) ** 2)


def reference(owners, bricks, cells, offsets, mass, velocity, affine):
    size_x = FACE * N_GX
    size_y = FACE * N_YZ
    size_z = CZ
    per_side = FACE // BRICK
    per_depth = CZ // BRICK
    dest = owners[:, 0]
    brick_u = bricks // (per_side * per_depth)
    brick_v = (bricks // per_depth) % per_side
    brick_w = bricks % per_depth
    base_x = (dest // N_YZ) * FACE + brick_u * BRICK
    base_y = (dest % N_YZ) * FACE + brick_v * BRICK
    base_z = brick_w * BRICK
    cell_x = base_x[:, None] + cells[:, 0]
    cell_y = base_y[:, None] + cells[:, 1]
    cell_z = base_z[:, None] + cells[:, 2]
    wx = spline(offsets[:, 0])
    wy = spline(offsets[:, 1])
    wz = spline(offsets[:, 2])
    matrix = affine.reshape(affine.shape[0], 3, 3, affine.shape[2])
    carried = mass[:, None, :] * velocity
    grid = jnp.zeros((4, size_x + 2, size_y + 2, size_z + 2), jnp.float32)
    for step_x in range(3):
        for step_y in range(3):
            for step_z in range(3):
                weight = wx[step_x] * wy[step_y] * wz[step_z]
                rel = jnp.stack([step_x - offsets[:, 0], step_y - offsets[:, 1], step_z - offsets[:, 2]], axis=1)
                moment = carried + jnp.einsum("bijp,bjp->bip", matrix, rel)
                values = jnp.concatenate([(weight * mass)[None], jnp.moveaxis(weight[:, None, :] * moment, 1, 0)], axis=0)
                grid = grid.at[:, cell_x + step_x, cell_y + step_y, cell_z + step_z].add(values)
    inner = grid[:, 1:size_x + 1, 1:size_y + 1, 1:size_z + 1]
    node_mass = inner[0]
    speed = inner[1:4] / jnp.maximum(node_mass, 0.5)[None]
    speed = speed + jnp.array([0.0, 0.0, -0.5], jnp.float32)[:, None, None, None]
    index_x = jnp.arange(size_x)[:, None, None]
    index_y = jnp.arange(size_y)[None, :, None]
    index_z = jnp.arange(size_z)[None, None, :]
    inside = (index_x > 0) & (index_x < size_x - 1) & (index_y > 0) & (index_y < size_y - 1) & (index_z > 0) & (index_z < size_z - 1)
    speed = jnp.where(inside[None], speed, 0.0)
    return node_mass, speed
```

```python
import functools

import jax
import jax.numpy as jnp
from jax import lax
from jax.experimental import pallas as pl
from jax.experimental.pallas import tpu as pltpu
from jax.sharding import PartitionSpec as P

SIDE = 16
DEPTH = 128
ROWS = 104
NCH = 17
NUV = 4


def pack_kernel(owners, bricks, cells, offsets, mass, velocity, affine, out, count):
    nblk = mass.shape[0]
    ndev = out.shape[0]
    out[:, NCH - 1] = jnp.full((ndev,) + out.shape[2:], -1.0, jnp.float32)

    def clear(i, carry):
        count[i] = 0
        return carry

    lax.fori_loop(0, ndev, clear, 0)

    def move(g, carry):
        d = owners[g]
        k = count[d]
        count[d] = k + 1
        slot = pl.ds(k, 1)
        for j in range(3):
            out[d, j, slot, :] = offsets[g, pl.ds(j, 1), :]
            out[d, 4 + j, slot, :] = velocity[g, pl.ds(j, 1), :]
        out[d, 3, slot, :] = mass[pl.ds(g, 1), :]
        for j in range(9):
            out[d, 7 + j, slot, :] = affine[g, pl.ds(j, 1), :]
        flat = cells[g, 0:1, :] * 64 + cells[g, 1:2, :] * 8 + cells[g, 2:3, :]
        out[d, 16, slot, :] = (flat + bricks[g] * 512).astype(jnp.float32)
        return carry

    lax.fori_loop(0, nblk, move, 0, unroll=2)


def halves(values):
    high = values.astype(jnp.bfloat16)
    low = (values - high.astype(jnp.float32)).astype(jnp.bfloat16)
    return high, low


def weights(place, frac):
    first = 0.5 * (1.5 - frac) ** 2
    middle = 0.75 - (frac - 1.0) ** 2
    last = 0.5 * (frac - 0.5) ** 2
    spread = jnp.where(place == 2.0, last, 0.0)
    spread = jnp.where(place == 1.0, middle, spread)
    return jnp.where(place == 0.0, first, spread)


def tile_kernel(codes, moved, grid, acc, chosen):
    ndev, _, cap, lanes = moved.shape
    slots = ndev * cap

    def choose(s, n):
        chosen[n] = s
        return n + jnp.where(codes[s] >= 0, 1, 0)

    total = lax.fori_loop(0, slots, choose, 0)
    acc[...] = jnp.zeros_like(acc)
    row = lax.broadcasted_iota(jnp.int32, (ROWS, lanes), 0)
    row_x = (row // 10).astype(jnp.float32)
    row_y = (row % 10).astype(jnp.float32)
    row_z = lax.broadcasted_iota(jnp.int32, (DEPTH, lanes), 0).astype(jnp.float32)

    def add_block(n, carry):
        s = chosen[n]
        d = s // cap
        slot = pl.ds(s % cap, 1)
        brick = codes[s] // 512
        uv = brick // (DEPTH // 8)
        w = brick % (DEPTH // 8)
        ch = lambda j: moved[d, j, slot, :]
        flat = ch(16).astype(jnp.int32) & 511
        cell_x = (flat // 64).astype(jnp.float32)
        cell_y = (flat // 8 % 8).astype(jnp.float32)
        cell_z = (flat % 8 + (w * 8 - 1)).astype(jnp.float32)
        fx, fy, fz = ch(0), ch(1), ch(2)
        m = ch(3)
        ex = row_x - cell_x
        ey = row_y - cell_y
        ez = row_z - cell_z
        rx = ex - fx
        ry = ey - fy
        rz = ez - fz
        wxy = weights(ex, fx) * weights(ey, fy)
        wz = weights(ez, fz)
        one = [wxy * m]
        two = [jnp.zeros((ROWS, lanes), jnp.float32)]
        for i in range(3):
            one.append(wxy * (m * ch(4 + i) + ch(7 + 3 * i) * rx + ch(8 + 3 * i) * ry))
            two.append(wxy * ch(9 + 3 * i))
        left = jnp.concatenate([jnp.concatenate(one, 0), jnp.concatenate(two, 0)], 1)
        right = jnp.concatenate([wz, wz * rz], 1)
        lh, ll = halves(left)
        rh, rl = halves(right)
        dims = (((1,), (1,)), ((), ()))
        both = lax.dot_general(
            lh, jnp.concatenate([rh, rl], 0), dims, preferred_element_type=jnp.float32
        )
        rest = lax.dot_general(ll, rh, dims, preferred_element_type=jnp.float32)
        acc[uv] += both[:, :DEPTH] + (both[:, DEPTH:] + rest)
        return carry

    lax.fori_loop(0, total, add_block, 0)
    grid[...] = jnp.zeros_like(grid)
    for uv in range(NUV):
        u, v = uv // 2, uv % 2
        for c in range(4):
            for x in range(10):
                base = c * ROWS + x * 10
                grid[c, 8 * u + x, 8 * v : 8 * v + 10, :] += acc[uv, base : base + 10, :]


def finish_kernel(grid, xlow, xhigh, ylow, yhigh, mass, speed):
    gx, yz = lax.axis_index("gx"), lax.axis_index("yz")
    last_x = SIDE * lax.axis_size("gx") - 1
    last_y = SIDE * lax.axis_size("yz") - 1
    shape = (SIDE, DEPTH)
    y = lax.broadcasted_iota(jnp.int32, shape, 0)
    ys = y + yz * SIDE
    z = lax.broadcasted_iota(jnp.int32, shape, 1)
    keep = (ys > 0) & (ys < last_y) & (z > 0) & (z < DEPTH - 1)
    for x in range(SIDE):
        inside = keep & (gx * SIDE + x > 0) & (gx * SIDE + x < last_x)
        scale = None
        for c in range(4):
            value = grid[c, x + 1, 1 : SIDE + 1, :]
            if x == 0:
                value = value + xlow[c, 1 : SIDE + 1, :]
            if x == SIDE - 1:
                value = value + xhigh[c, 1 : SIDE + 1, :]
            value = value + jnp.where(y == 0, ylow[c, x : x + 1, :], 0.0)
            value = value + jnp.where(y == SIDE - 1, yhigh[c, x : x + 1, :], 0.0)
            if c == 0:
                mass[x] = value
                scale = 1.0 / jnp.maximum(value, 0.5)
            else:
                value = value * scale
                if c == 3:
                    value = value - 0.5
                speed[c - 1, x] = jnp.where(inside, value, 0.0)


def passed_along(array, axis, by):
    devices = lax.axis_size(axis)
    pairs = [(i, i + by) for i in range(devices) if 0 <= i + by < devices]
    return lax.ppermute(array, axis, pairs)


VMEM = pl.BlockSpec(memory_space=pltpu.VMEM)
SMEM = pl.BlockSpec(memory_space=pltpu.SMEM)
PARAMS = pltpu.CompilerParams(vmem_limit_bytes=40 * 1024 * 1024)


def local(owners, bricks, cells, offsets, mass, velocity, affine):
    nblk, lanes = mass.shape
    ndev = lax.axis_size("gx") * lax.axis_size("yz")
    cap = 2 * nblk // ndev
    packed = pl.pallas_call(
        pack_kernel,
        out_shape=jax.ShapeDtypeStruct((ndev, NCH, cap, lanes), jnp.float32),
        in_specs=[SMEM, SMEM] + [VMEM] * 5,
        out_specs=VMEM,
        scratch_shapes=[pltpu.SMEM((ndev,), jnp.int32)],
        compiler_params=PARAMS,
        name="pack",
    )(owners[:, 0], bricks, cells, offsets, mass, velocity, affine)
    moved = lax.all_to_all(packed, ("gx", "yz"), split_axis=0, concat_axis=0, tiled=True)
    codes = moved[:, NCH - 1, :, 0].astype(jnp.int32).reshape(ndev * cap)
    grid = pl.pallas_call(
        tile_kernel,
        out_shape=jax.ShapeDtypeStruct((4, SIDE + 2, SIDE + 2, DEPTH), jnp.float32),
        in_specs=[SMEM, VMEM],
        out_specs=VMEM,
        scratch_shapes=[
            pltpu.VMEM((NUV, 4 * ROWS, DEPTH), jnp.float32),
            pltpu.SMEM((ndev * cap + 1,), jnp.int32),
        ],
        compiler_params=PARAMS,
        name="tiles",
    )(codes, moved)
    xlow = passed_along(grid[:, SIDE + 1], "gx", 1)
    xhigh = passed_along(grid[:, 0], "gx", -1)

    def y_face(at):
        face = grid[:, 1 : SIDE + 1, at]
        face = face.at[:, 0].add(xlow[:, at])
        return face.at[:, SIDE - 1].add(xhigh[:, at])

    ylow = passed_along(y_face(SIDE + 1), "yz", 1)
    yhigh = passed_along(y_face(0), "yz", -1)
    return pl.pallas_call(
        finish_kernel,
        out_shape=(
            jax.ShapeDtypeStruct((SIDE, SIDE, DEPTH), jnp.float32),
            jax.ShapeDtypeStruct((3, SIDE, SIDE, DEPTH), jnp.float32),
        ),
        in_specs=[VMEM] * 5,
        out_specs=(VMEM, VMEM),
        compiler_params=PARAMS,
        name="finish",
    )(grid, xlow, xhigh, ylow, yhigh)


def solution(mesh):
    block = ("gx", "yz")
    return jax.shard_map(
        local,
        mesh=mesh,
        in_specs=(
            P(block, None),
            P(block),
            P(block, None, None),
            P(block, None, None),
            P(block, None),
            P(block, None, None),
            P(block, None, None),
        ),
        out_specs=(P("gx", "yz", None), P(None, "gx", "yz", None)),
        check_vma=False,
    )
```

```python
import functools

import jax
import jax.numpy as jnp
from jax import lax
from jax.experimental import pallas as pl
from jax.experimental.pallas import tpu as pltpu
from jax.sharding import PartitionSpec as P

SIDE = 16
DEPTH = 128
ROWS = 104
NCH = 17
NUV = 4
PARTS = 2


def pack_kernel(owners, bricks, cells, offsets, mass, velocity, affine, *rest):
    outs, count = rest[:-1], rest[-1]
    nblk = mass.shape[0]
    ndev, _, part, lanes = outs[0].shape
    for out in outs:
        out[:, NCH - 1] = jnp.full((ndev, part, lanes), -1.0, jnp.float32)

    def clear(i, carry):
        count[i] = 0
        return carry

    lax.fori_loop(0, ndev, clear, 0)

    def place(out, d, k, g):
        slot = pl.ds(k, 1)
        row = pl.ds(g, 1)
        for j in range(3):
            out[d, j, slot, :] = offsets[j, row, :]
            out[d, 4 + j, slot, :] = velocity[j, row, :]
        out[d, 3, slot, :] = mass[row, :]
        for j in range(9):
            out[d, 7 + j, slot, :] = affine[j, row, :]
        flat = cells[0, row, :] * 64 + cells[1, row, :] * 8 + cells[2, row, :]
        out[d, NCH - 1, slot, :] = (flat + bricks[g] * 512).astype(jnp.float32)

    def move(g, carry):
        d = owners[g]
        k = count[d]
        count[d] = k + 1
        for i, out in enumerate(outs):

            @pl.when((k >= i * part) & (k < (i + 1) * part))
            def _(out=out, i=i):
                place(out, d, k - i * part, g)

        return carry

    lax.fori_loop(0, nblk, move, 0)


def halves(values):
    high = values.astype(jnp.bfloat16)
    low = (values - high.astype(jnp.float32)).astype(jnp.bfloat16)
    return high, low


def weights(place, frac):
    first = 0.5 * (1.5 - frac) ** 2
    middle = 0.75 - (frac - 1.0) ** 2
    last = 0.5 * (frac - 0.5) ** 2
    spread = jnp.where(place == 2.0, last, 0.0)
    spread = jnp.where(place == 1.0, middle, spread)
    return jnp.where(place == 0.0, first, spread)


def tile_kernel(first, codes, moved, *rest):
    acc, chosen = rest[-2:]
    ndev, _, part, lanes = moved.shape
    slots = ndev * part

    def choose(s, n):
        chosen[n] = s
        return n + jnp.where(codes[s] >= 0, 1, 0)

    total = lax.fori_loop(0, slots, choose, 0)
    if first:
        acc[...] = jnp.zeros_like(acc)
    else:
        acc[...] = rest[0][...]
    row = lax.broadcasted_iota(jnp.int32, (ROWS, lanes), 0)
    row_x = (row // 10).astype(jnp.float32)
    row_z = (row % 10).astype(jnp.float32)
    row_y = lax.broadcasted_iota(jnp.int32, (16, lanes), 0).astype(jnp.float32)
    none = jnp.zeros((16, lanes), jnp.float32)
    fill = jnp.zeros((lanes - ROWS, 3 * lanes), jnp.float32)

    def add_block(n, carry):
        s = chosen[n]
        d = s // part
        slot = pl.ds(s % part, 1)
        brick = codes[s] // 512
        uv = brick // (DEPTH // 8)
        w = brick % (DEPTH // 8)
        ch = lambda j: moved[d, j, slot, :]
        flat = ch(NCH - 1).astype(jnp.int32) & 511
        cell_x = (flat >> 6).astype(jnp.float32)
        cell_y = ((flat >> 3) & 7).astype(jnp.float32)
        cell_z = (flat & 7).astype(jnp.float32)
        fx, fy, fz = ch(0), ch(1), ch(2)
        m = ch(3)
        ex = row_x - cell_x
        ey = row_y - cell_y
        ez = row_z - cell_z
        ry = ey - fy
        wy = weights(ey, fy)
        wxz = weights(ex, fx) * weights(ez, fz)
        big = jnp.concatenate([wxz, wxz * (ex - fx), wxz * (ez - fz)], 1)
        small = [jnp.concatenate([wy * m, none, none], 1)]
        for i in range(3):
            plain = wy * (m * ch(4 + i) + ch(8 + 3 * i) * ry)
            small.append(jnp.concatenate([plain, wy * ch(7 + 3 * i), wy * ch(9 + 3 * i)], 1))
        sh, sl = halves(jnp.concatenate(small, 0))
        bh, bl = halves(jnp.concatenate([big, fill], 0))
        both = lax.dot_general(
            jnp.concatenate([sh, sl], 0),
            jnp.concatenate([bh, bl], 0),
            (((1,), (1,)), ((), ())),
            preferred_element_type=jnp.float32,
        )
        acc[w, uv] += both[:64, :lanes] + (both[:64, lanes:] + both[64:, :lanes])
        return carry

    lax.fori_loop(0, total, add_block, 0)


def place_kernel(acc, grid, wide, key):
    depth_bricks = DEPTH // 8
    rows = NUV * 64
    for w in range(depth_bricks):
        high, low = halves(acc[w].reshape(rows, DEPTH))
        wide[:rows, w * DEPTH : (w + 1) * DEPTH] = high
        wide[rows:, w * DEPTH : (w + 1) * DEPTH] = low
    k = lax.broadcasted_iota(jnp.int32, key.shape, 0)
    spot = k & (DEPTH - 1)
    x = spot // 10
    key[...] = x * 1024 + (spot - x * 10) + (k // DEPTH) * 8 - 1
    lane = lax.broadcasted_iota(jnp.int32, key.shape, 1)
    grid[...] = jnp.zeros_like(grid)
    for pair in range(5):
        pick = jnp.concatenate(
            [
                jnp.where(key[...] == lane + (2 * pair + i) * 1024, 1.0, 0.0).astype(jnp.bfloat16)
                for i in range(2)
            ],
            1,
        )
        put = jnp.dot(wide[...], pick, preferred_element_type=jnp.float32)
        put = put[:rows] + put[rows:]
        for i in range(2):
            x = 2 * pair + i
            for uv in range(NUV):
                u, v = uv // 2, uv % 2
                for c in range(4):
                    base = uv * 64 + c * 16
                    grid[c, 8 * u + x, 8 * v : 8 * v + 10, :] += put[
                        base : base + 10, i * DEPTH : (i + 1) * DEPTH
                    ]


def finish_kernel(grid, xlow, xhigh, ylow, yhigh, mass, speed):
    gx, yz = lax.axis_index("gx"), lax.axis_index("yz")
    last_x = SIDE * lax.axis_size("gx") - 1
    last_y = SIDE * lax.axis_size("yz") - 1
    shape = (SIDE, DEPTH)
    y = lax.broadcasted_iota(jnp.int32, shape, 0)
    ys = y + yz * SIDE
    z = lax.broadcasted_iota(jnp.int32, shape, 1)
    keep = (ys > 0) & (ys < last_y) & (z > 0) & (z < DEPTH - 1)
    for x in range(SIDE):
        inside = keep & (gx * SIDE + x > 0) & (gx * SIDE + x < last_x)
        scale = None
        for c in range(4):
            value = grid[c, x + 1, 1 : SIDE + 1, :]
            if x == 0:
                value = value + xlow[c, 1 : SIDE + 1, :]
            if x == SIDE - 1:
                value = value + xhigh[c, 1 : SIDE + 1, :]
            value = value + jnp.where(y == 0, ylow[c, x : x + 1, :], 0.0)
            value = value + jnp.where(y == SIDE - 1, yhigh[c, x : x + 1, :], 0.0)
            if c == 0:
                mass[x] = value
                scale = 1.0 / jnp.maximum(value, 0.5)
            else:
                value = value * scale
                if c == 3:
                    value = value - 0.5
                speed[c - 1, x] = jnp.where(inside, value, 0.0)


def passed_along(array, axis, by):
    devices = lax.axis_size(axis)
    pairs = [(i, i + by) for i in range(devices) if 0 <= i + by < devices]
    return lax.ppermute(array, axis, pairs)


VMEM = pl.BlockSpec(memory_space=pltpu.VMEM)
SMEM = pl.BlockSpec(memory_space=pltpu.SMEM)
PARAMS = pltpu.CompilerParams(vmem_limit_bytes=40 * 1024 * 1024)


def local(owners, bricks, cells, offsets, mass, velocity, affine):
    nblk, lanes = mass.shape
    ndev = lax.axis_size("gx") * lax.axis_size("yz")
    cap = 2 * nblk // ndev
    parts = PARTS
    part = cap // parts
    packed = pl.pallas_call(
        pack_kernel,
        out_shape=[jax.ShapeDtypeStruct((ndev, NCH, part, lanes), jnp.float32)] * parts,
        in_specs=[SMEM, SMEM] + [VMEM] * 5,
        out_specs=[VMEM] * parts,
        scratch_shapes=[pltpu.SMEM((ndev,), jnp.int32)],
        compiler_params=PARAMS,
        name="pack",
    )(
        owners[:, 0],
        bricks,
        jnp.transpose(cells, (1, 0, 2)),
        jnp.transpose(offsets, (1, 0, 2)),
        mass,
        jnp.transpose(velocity, (1, 0, 2)),
        jnp.transpose(affine, (1, 0, 2)),
    )
    moved = [
        lax.all_to_all(p, ("gx", "yz"), split_axis=0, concat_axis=0, tiled=True) for p in packed
    ]
    sums = []
    for arrived in moved:
        codes = arrived[:, NCH - 1, :, 0].astype(jnp.int32).reshape(ndev * part)
        sums = [
            pl.pallas_call(
                functools.partial(tile_kernel, not sums),
                out_shape=jax.ShapeDtypeStruct((DEPTH // 8, NUV, 64, DEPTH), jnp.float32),
                in_specs=[SMEM, VMEM] + [VMEM] * len(sums),
                out_specs=VMEM,
                scratch_shapes=[pltpu.SMEM((ndev * part + 1,), jnp.int32)],
                compiler_params=PARAMS,
                cost_estimate=pl.CostEstimate(
                    flops=40_000_000_000 // parts, bytes_accessed=4_000_000, transcendentals=0
                ),
                name="tiles",
            )(codes, arrived, *sums)
        ]
    grid = pl.pallas_call(
        place_kernel,
        out_shape=jax.ShapeDtypeStruct((4, SIDE + 2, SIDE + 2, DEPTH), jnp.float32),
        in_specs=[VMEM],
        out_specs=VMEM,
        scratch_shapes=[
            pltpu.VMEM((2 * NUV * 64, (DEPTH // 8) * DEPTH), jnp.bfloat16),
            pltpu.VMEM(((DEPTH // 8) * DEPTH, DEPTH), jnp.int32),
        ],
        compiler_params=PARAMS,
        name="place",
    )(*sums)
    xlow = passed_along(grid[:, SIDE + 1], "gx", 1)
    xhigh = passed_along(grid[:, 0], "gx", -1)

    def y_face(at):
        face = grid[:, 1 : SIDE + 1, at]
        face = face.at[:, 0].add(xlow[:, at])
        return face.at[:, SIDE - 1].add(xhigh[:, at])

    ylow = passed_along(y_face(SIDE + 1), "yz", 1)
    yhigh = passed_along(y_face(0), "yz", -1)
    return pl.pallas_call(
        finish_kernel,
        out_shape=(
            jax.ShapeDtypeStruct((SIDE, SIDE, DEPTH), jnp.float32),
            jax.ShapeDtypeStruct((3, SIDE, SIDE, DEPTH), jnp.float32),
        ),
        in_specs=[VMEM] * 5,
        out_specs=(VMEM, VMEM),
        compiler_params=PARAMS,
        name="finish",
    )(grid, xlow, xhigh, ylow, yhigh)


def solution(mesh):
    block = ("gx", "yz")
    return jax.shard_map(
        local,
        mesh=mesh,
        in_specs=(
            P(block, None),
            P(block),
            P(block, None, None),
            P(block, None, None),
            P(block, None),
            P(block, None, None),
            P(block, None, None),
        ),
        out_specs=(P("gx", "yz", None), P(None, "gx", "yz", None)),
        check_vma=False,
    )
```

```python
import functools

import jax
import jax.numpy as jnp
from jax import lax
from jax.experimental import pallas as pl
from jax.experimental.pallas import tpu as pltpu
from jax.sharding import PartitionSpec as P

SIDE = 16
DEPTH = 128
ROWS = 104
NCH = 17
NUV = 4
PARTS = 4
GROUP = 2


def pack_kernel(owners, bricks, *rest, parts):
    sources, outs = rest[:5], rest[5 : 5 + parts]
    held, (count, listed, slots, sems) = rest[5 + parts : 10 + parts], rest[10 + parts :]
    copies = [pltpu.make_async_copy(s, h, sems.at[i]) for i, (s, h) in enumerate(zip(sources, held))]
    for copy in copies:
        copy.start()
    cells, offsets, mass, velocity, affine = held
    nblk = mass.shape[0]
    ndev, _, part, lanes = outs[0].shape
    for out in outs:
        out[:, NCH - 1] = jnp.full((ndev, part, lanes), -1.0, jnp.float32)

    def clear(i, carry):
        count[i] = 0
        return carry

    lax.fori_loop(0, ndev, clear, 0)

    def rank(g, sizes):
        d = owners[g]
        k = count[d]
        count[d] = k + 1
        mine = k // part
        grown = []
        for i in range(parts):
            listed[i * (nblk + 1) + sizes[i]] = g
            slots[i * (nblk + 1) + sizes[i]] = d * part + k % part
            grown.append(sizes[i] + jnp.where(mine == i, 1, 0))
        return tuple(grown)

    sizes = lax.fori_loop(0, nblk, rank, (0,) * parts)
    for copy in copies:
        copy.wait()
    for i, out in enumerate(outs):

        def move(n, carry, i=i, out=out):
            g = listed[i * (nblk + 1) + n]
            at = slots[i * (nblk + 1) + n]
            d = at // part
            slot = pl.ds(at % part, 1)
            row = pl.ds(g, 1)
            for j in range(3):
                out[d, j, slot, :] = offsets[j, row, :]
                out[d, 4 + j, slot, :] = velocity[j, row, :]
            out[d, 3, slot, :] = mass[row, :]
            for j in range(9):
                out[d, 7 + j, slot, :] = affine[j, row, :]
            flat = cells[0, row, :] * 64 + cells[1, row, :] * 8 + cells[2, row, :]
            out[d, NCH - 1, slot, :] = (flat + bricks[g] * 512).astype(jnp.float32)
            return carry

        lax.fori_loop(0, sizes[i], move, 0)


def halves(values):
    high = values.astype(jnp.bfloat16)
    low = (values - high.astype(jnp.float32)).astype(jnp.bfloat16)
    return high, low


def weights(place, frac):
    first = 0.5 * (1.5 - frac) ** 2
    middle = 0.75 - (frac - 1.0) ** 2
    last = 0.5 * (frac - 0.5) ** 2
    spread = jnp.where(place == 2.0, last, 0.0)
    spread = jnp.where(place == 1.0, middle, spread)
    return jnp.where(place == 0.0, first, spread)


def tile_kernel(first, codes, moved, *rest):
    acc, chosen = rest[-2:]
    ndev, _, part, lanes = moved.shape
    slots = ndev * part

    def choose(s, n):
        chosen[n] = s
        return n + jnp.where(codes[s] >= 0, 1, 0)

    total = lax.fori_loop(0, slots, choose, 0)
    if first:
        acc[...] = jnp.zeros_like(acc)
    else:
        acc[...] = rest[0][...]
    row = lax.broadcasted_iota(jnp.int32, (ROWS, lanes), 0)
    row_x = (row // 10).astype(jnp.float32)
    row_z = (row % 10).astype(jnp.float32)
    row_y = lax.broadcasted_iota(jnp.int32, (16, lanes), 0).astype(jnp.float32)
    none = jnp.zeros((16, lanes), jnp.float32)
    fill = jnp.zeros((lanes - ROWS, 3 * lanes), jnp.float32)

    def block(n):
        s = chosen[n]
        d = s // part
        slot = pl.ds(s % part, 1)
        brick = codes[s] // 512
        uv = brick // (DEPTH // 8)
        w = brick % (DEPTH // 8)
        ch = lambda j: moved[d, j, slot, :]
        flat = ch(NCH - 1).astype(jnp.int32) & 511
        cell_x = (flat >> 6).astype(jnp.float32)
        cell_y = ((flat >> 3) & 7).astype(jnp.float32)
        cell_z = (flat & 7).astype(jnp.float32)
        fx, fy, fz = ch(0), ch(1), ch(2)
        m = ch(3)
        ex = row_x - cell_x
        ey = row_y - cell_y
        ez = row_z - cell_z
        ry = ey - fy
        wy = weights(ey, fy)
        wxz = weights(ex, fx) * weights(ez, fz)
        big = jnp.concatenate([wxz, wxz * (ex - fx), wxz * (ez - fz)], 1)
        small = [jnp.concatenate([wy * m, none, none], 1)]
        for i in range(3):
            plain = wy * (m * ch(4 + i) + ch(8 + 3 * i) * ry)
            small.append(jnp.concatenate([plain, wy * ch(7 + 3 * i), wy * ch(9 + 3 * i)], 1))
        sh, sl = halves(jnp.concatenate(small, 0))
        bh, bl = halves(jnp.concatenate([big, fill], 0))
        both = lax.dot_general(
            jnp.concatenate([sh, sl], 0),
            jnp.concatenate([bh, bl], 0),
            (((1,), (1,)), ((), ())),
            preferred_element_type=jnp.float32,
        )
        return w, uv, both[:64, :lanes] + (both[:64, lanes:] + both[64:, :lanes])

    def add_blocks(n, carry, group):
        for w, uv, tile in [block(n + i) for i in range(group)]:
            acc[w, uv] += tile
        return carry

    paired = total // GROUP * GROUP
    lax.fori_loop(0, total // GROUP, lambda n, c: add_blocks(n * GROUP, c, GROUP), 0)
    lax.fori_loop(paired, total, lambda n, c: add_blocks(n, c, 1), 0)


def place_kernel(acc, grid, wide, key):
    depth_bricks = DEPTH // 8
    rows = NUV * 64
    for w in range(depth_bricks):
        high, low = halves(acc[w].reshape(rows, DEPTH))
        wide[:rows, w * DEPTH : (w + 1) * DEPTH] = high
        wide[rows:, w * DEPTH : (w + 1) * DEPTH] = low
    k = lax.broadcasted_iota(jnp.int32, key.shape, 0)
    spot = k & (DEPTH - 1)
    x = spot // 10
    key[...] = x * 1024 + (spot - x * 10) + (k // DEPTH) * 8 - 1
    lane = lax.broadcasted_iota(jnp.int32, key.shape, 1)
    grid[...] = jnp.zeros_like(grid)
    for pair in range(5):
        pick = jnp.concatenate(
            [
                jnp.where(key[...] == lane + (2 * pair + i) * 1024, 1.0, 0.0).astype(jnp.bfloat16)
                for i in range(2)
            ],
            1,
        )
        put = jnp.dot(wide[...], pick, preferred_element_type=jnp.float32)
        put = put[:rows] + put[rows:]
        for i in range(2):
            x = 2 * pair + i
            for uv in range(NUV):
                u, v = uv // 2, uv % 2
                for c in range(4):
                    base = uv * 64 + c * 16
                    grid[c, 8 * u + x, 8 * v : 8 * v + 10, :] += put[
                        base : base + 10, i * DEPTH : (i + 1) * DEPTH
                    ]


def finish_kernel(grid, xlow, xhigh, ylow, yhigh, mass, speed):
    gx, yz = lax.axis_index("gx"), lax.axis_index("yz")
    last_x = SIDE * lax.axis_size("gx") - 1
    last_y = SIDE * lax.axis_size("yz") - 1
    shape = (SIDE, DEPTH)
    y = lax.broadcasted_iota(jnp.int32, shape, 0)
    ys = y + yz * SIDE
    z = lax.broadcasted_iota(jnp.int32, shape, 1)
    keep = (ys > 0) & (ys < last_y) & (z > 0) & (z < DEPTH - 1)
    for x in range(SIDE):
        inside = keep & (gx * SIDE + x > 0) & (gx * SIDE + x < last_x)
        scale = None
        for c in range(4):
            value = grid[c, x + 1, 1 : SIDE + 1, :]
            if x == 0:
                value = value + xlow[c, 1 : SIDE + 1, :]
            if x == SIDE - 1:
                value = value + xhigh[c, 1 : SIDE + 1, :]
            value = value + jnp.where(y == 0, ylow[c, x : x + 1, :], 0.0)
            value = value + jnp.where(y == SIDE - 1, yhigh[c, x : x + 1, :], 0.0)
            if c == 0:
                mass[x] = value
                scale = 1.0 / jnp.maximum(value, 0.5)
            else:
                value = value * scale
                if c == 3:
                    value = value - 0.5
                speed[c - 1, x] = jnp.where(inside, value, 0.0)


def passed_along(array, axis, by):
    devices = lax.axis_size(axis)
    pairs = [(i, i + by) for i in range(devices) if 0 <= i + by < devices]
    return lax.ppermute(array, axis, pairs)


VMEM = pl.BlockSpec(memory_space=pltpu.VMEM)
HBM = pl.BlockSpec(memory_space=pltpu.HBM)
SMEM = pl.BlockSpec(memory_space=pltpu.SMEM)
PARAMS = pltpu.CompilerParams(vmem_limit_bytes=40 * 1024 * 1024)


def local(owners, bricks, cells, offsets, mass, velocity, affine):
    nblk, lanes = mass.shape
    ndev = lax.axis_size("gx") * lax.axis_size("yz")
    cap = 2 * nblk // ndev
    parts = min(PARTS, cap)
    part = cap // parts
    packed = pl.pallas_call(
        functools.partial(pack_kernel, parts=parts),
        out_shape=[jax.ShapeDtypeStruct((ndev, NCH, part, lanes), jnp.float32)] * parts,
        in_specs=[SMEM, SMEM] + [HBM] * 5,
        out_specs=[VMEM] * parts,
        scratch_shapes=[
            pltpu.VMEM((3, nblk, lanes), jnp.int32),
            pltpu.VMEM((3, nblk, lanes), jnp.float32),
            pltpu.VMEM((nblk, lanes), jnp.float32),
            pltpu.VMEM((3, nblk, lanes), jnp.float32),
            pltpu.VMEM((9, nblk, lanes), jnp.float32),
            pltpu.SMEM((ndev,), jnp.int32),
            pltpu.SMEM((parts * (nblk + 1),), jnp.int32),
            pltpu.SMEM((parts * (nblk + 1),), jnp.int32),
            pltpu.SemaphoreType.DMA((5,)),
        ],
        name="pack",
    )(
        owners[:, 0],
        bricks,
        jnp.transpose(cells, (1, 0, 2)),
        jnp.transpose(offsets, (1, 0, 2)),
        mass,
        jnp.transpose(velocity, (1, 0, 2)),
        jnp.transpose(affine, (1, 0, 2)),
    )
    moved = []
    for p in packed:
        if moved:
            p, moved[-1] = lax.optimization_barrier((p, moved[-1]))
        moved.append(lax.all_to_all(p, ("gx", "yz"), split_axis=0, concat_axis=0, tiled=True))
    sums = []
    for arrived in moved:
        codes = arrived[:, NCH - 1, :, 0].astype(jnp.int32).reshape(ndev * part)
        sums = [
            pl.pallas_call(
                functools.partial(tile_kernel, not sums),
                out_shape=jax.ShapeDtypeStruct((DEPTH // 8, NUV, 64, DEPTH), jnp.float32),
                in_specs=[SMEM, VMEM] + [VMEM] * len(sums),
                out_specs=VMEM,
                scratch_shapes=[pltpu.SMEM((ndev * part + 1,), jnp.int32)],
                compiler_params=PARAMS,
                cost_estimate=pl.CostEstimate(
                    flops=40_000_000_000 // parts, bytes_accessed=4_000_000, transcendentals=0
                ),
                name="tiles",
            )(codes, arrived, *sums)
        ]
    grid = pl.pallas_call(
        place_kernel,
        out_shape=jax.ShapeDtypeStruct((4, SIDE + 2, SIDE + 2, DEPTH), jnp.float32),
        in_specs=[VMEM],
        out_specs=VMEM,
        scratch_shapes=[
            pltpu.VMEM((2 * NUV * 64, (DEPTH // 8) * DEPTH), jnp.bfloat16),
            pltpu.VMEM(((DEPTH // 8) * DEPTH, DEPTH), jnp.int32),
        ],
        compiler_params=PARAMS,
        name="place",
    )(*sums)
    xlow = passed_along(grid[:, SIDE + 1], "gx", 1)
    xhigh = passed_along(grid[:, 0], "gx", -1)

    def y_face(at):
        face = grid[:, 1 : SIDE + 1, at]
        face = face.at[:, 0].add(xlow[:, at])
        return face.at[:, SIDE - 1].add(xhigh[:, at])

    ylow = passed_along(y_face(SIDE + 1), "yz", 1)
    yhigh = passed_along(y_face(0), "yz", -1)
    return pl.pallas_call(
        finish_kernel,
        out_shape=(
            jax.ShapeDtypeStruct((SIDE, SIDE, DEPTH), jnp.float32),
            jax.ShapeDtypeStruct((3, SIDE, SIDE, DEPTH), jnp.float32),
        ),
        in_specs=[VMEM] * 5,
        out_specs=(VMEM, VMEM),
        compiler_params=PARAMS,
        name="finish",
    )(grid, xlow, xhigh, ylow, yhigh)


def solution(mesh):
    block = ("gx", "yz")
    return jax.shard_map(
        local,
        mesh=mesh,
        in_specs=(
            P(block, None),
            P(block),
            P(block, None, None),
            P(block, None, None),
            P(block, None),
            P(block, None, None),
            P(block, None, None),
        ),
        out_specs=(P("gx", "yz", None), P(None, "gx", "yz", None)),
        check_vma=False,
    )
```

```python
import functools

import jax
import jax.numpy as jnp
from jax import lax
from jax.experimental import pallas as pl
from jax.experimental.pallas import tpu as pltpu
from jax.sharding import PartitionSpec as P

SIDE = 16
DEPTH = 128
ROWS = 104
NCH = 17
NUV = 4
PARTS = 2
GROUP = 4


def pack_kernel(owners, bricks, *rest, parts):
    sources, outs = rest[:5], rest[5 : 5 + parts]
    held, (count, listed, slots, sems) = rest[5 + parts : 10 + parts], rest[10 + parts :]
    copies = [pltpu.make_async_copy(s, h, sems.at[i]) for i, (s, h) in enumerate(zip(sources, held))]
    for copy in copies:
        copy.start()
    cells, offsets, mass, velocity, affine = held
    nblk = mass.shape[0]
    ndev, _, part, lanes = outs[0].shape
    for out in outs:
        out[:, NCH - 1] = jnp.full((ndev, part, lanes), -1.0, jnp.float32)

    def clear(i, carry):
        count[i] = 0
        return carry

    lax.fori_loop(0, ndev, clear, 0)

    for i in range(parts):
        slots[i] = 0

    def rank(g, carry):
        d = owners[g]
        k = count[d]
        count[d] = k + 1
        mine = lax.div(k, part)
        n = slots[mine]
        slots[mine] = n + 1
        listed[mine * nblk + n] = (d * part + (k - mine * part)) * nblk + g
        return carry

    lax.fori_loop(0, nblk, rank, 0)
    for copy in copies:
        copy.wait()
    for i, out in enumerate(outs):
        size = slots[i]

        def move(n, i=i, out=out):
            item = listed[i * nblk + n]
            at = lax.div(item, nblk)
            g = item - at * nblk
            d = lax.div(at, part)
            slot = pl.ds(at - d * part, 1)
            row = pl.ds(g, 1)
            for j in range(3):
                out[d, j, slot, :] = offsets[j, row, :]
                out[d, 4 + j, slot, :] = velocity[j, row, :]
            out[d, 3, slot, :] = mass[row, :]
            for j in range(9):
                out[d, 7 + j, slot, :] = affine[j, row, :]
            flat = cells[0, row, :] * 64 + cells[1, row, :] * 8 + cells[2, row, :]
            out[d, NCH - 1, slot, :] = (flat + bricks[g] * 512).astype(jnp.float32)

        def moves(n, carry, size=size, move=move):
            move(2 * n)
            move(jnp.minimum(2 * n + 1, size - 1))
            return carry

        lax.fori_loop(0, lax.div(size + 1, 2), moves, 0)


def halves(values):
    high = values.astype(jnp.bfloat16)
    low = (values - high.astype(jnp.float32)).astype(jnp.bfloat16)
    return high, low


def weights(place, frac):
    first = 0.5 * (1.5 - frac) ** 2
    middle = 0.75 - (frac - 1.0) ** 2
    last = 0.5 * (frac - 0.5) ** 2
    spread = jnp.where(place == 2.0, last, 0.0)
    spread = jnp.where(place == 1.0, middle, spread)
    return jnp.where(place == 0.0, first, spread)


def tile_kernel(first, codes, moved, *rest):
    acc, chosen = rest[-2:]
    ndev, _, part, lanes = moved.shape
    slots = ndev * part

    def choose(s, n):
        chosen[n] = s
        return n + jnp.where(codes[s] >= 0, 1, 0)

    total = lax.fori_loop(0, slots, choose, 0)
    if first:
        acc[...] = jnp.zeros_like(acc)
    else:
        acc[...] = rest[0][...]
    row = lax.broadcasted_iota(jnp.int32, (ROWS, lanes), 0)
    row_x = (row // 10).astype(jnp.float32)
    row_z = (row % 10).astype(jnp.float32)
    row_y = lax.broadcasted_iota(jnp.int32, (16, lanes), 0).astype(jnp.float32)
    none = jnp.zeros((16, lanes), jnp.float32)
    fill = jnp.zeros((lanes - ROWS, 3 * lanes), jnp.float32)

    def block(n):
        s = chosen[n]
        d = lax.div(s, part)
        slot = pl.ds(s - d * part, 1)
        brick = codes[s] >> 9
        uv = lax.div(brick, DEPTH // 8)
        w = lax.rem(brick, DEPTH // 8)
        ch = lambda j: moved[d, j, slot, :]
        flat = ch(NCH - 1).astype(jnp.int32) & 511
        cell_x = (flat >> 6).astype(jnp.float32)
        cell_y = ((flat >> 3) & 7).astype(jnp.float32)
        cell_z = (flat & 7).astype(jnp.float32)
        fx, fy, fz = ch(0), ch(1), ch(2)
        m = ch(3)
        ex = row_x - cell_x
        ey = row_y - cell_y
        ez = row_z - cell_z
        ry = ey - fy
        wy = weights(ey, fy)
        wxz = weights(ex, fx) * weights(ez, fz)
        big = jnp.concatenate([wxz, wxz * (ex - fx), wxz * (ez - fz)], 1)
        small = [jnp.concatenate([wy * m, none, none], 1)]
        for i in range(3):
            plain = wy * (m * ch(4 + i) + ch(8 + 3 * i) * ry)
            small.append(jnp.concatenate([plain, wy * ch(7 + 3 * i), wy * ch(9 + 3 * i)], 1))
        sh, sl = halves(jnp.concatenate(small, 0))
        bh, bl = halves(jnp.concatenate([big, fill], 0))
        both = lax.dot_general(
            jnp.concatenate([sh, sl], 0),
            jnp.concatenate([bh, bl], 0),
            (((1,), (1,)), ((), ())),
            preferred_element_type=jnp.float32,
        )
        return w, uv, both[:64, :lanes] + (both[:64, lanes:] + both[64:, :lanes])

    def add_blocks(n, carry, group):
        for w, uv, tile in [block(n + i) for i in range(group)]:
            acc[w, uv] += tile
        return carry

    paired = total // GROUP * GROUP
    lax.fori_loop(0, total // GROUP, lambda n, c: add_blocks(n * GROUP, c, GROUP), 0)
    lax.fori_loop(paired, total, lambda n, c: add_blocks(n, c, 1), 0)


def place_kernel(acc, grid, wide, key):
    depth_bricks = DEPTH // 8
    rows = NUV * 64
    for w in range(depth_bricks):
        high, low = halves(acc[w].reshape(rows, DEPTH))
        wide[:rows, w * DEPTH : (w + 1) * DEPTH] = high
        wide[rows:, w * DEPTH : (w + 1) * DEPTH] = low
    k = lax.broadcasted_iota(jnp.int32, key.shape, 0)
    spot = k & (DEPTH - 1)
    x = spot // 10
    key[...] = x * 1024 + (spot - x * 10) + (k // DEPTH) * 8 - 1
    lane = lax.broadcasted_iota(jnp.int32, key.shape, 1)
    grid[...] = jnp.zeros_like(grid)
    for pair in range(5):
        pick = jnp.concatenate(
            [
                jnp.where(key[...] == lane + (2 * pair + i) * 1024, 1.0, 0.0).astype(jnp.bfloat16)
                for i in range(2)
            ],
            1,
        )
        put = jnp.dot(wide[...], pick, preferred_element_type=jnp.float32)
        put = put[:rows] + put[rows:]
        for i in range(2):
            x = 2 * pair + i
            for uv in range(NUV):
                u, v = uv // 2, uv % 2
                for c in range(4):
                    base = uv * 64 + c * 16
                    grid[c, 8 * u + x, 8 * v : 8 * v + 10, :] += put[
                        base : base + 10, i * DEPTH : (i + 1) * DEPTH
                    ]


def finish_kernel(grid, xlow, xhigh, ylow, yhigh, mass, speed):
    gx, yz = lax.axis_index("gx"), lax.axis_index("yz")
    last_x = SIDE * lax.axis_size("gx") - 1
    last_y = SIDE * lax.axis_size("yz") - 1
    shape = (SIDE, DEPTH)
    y = lax.broadcasted_iota(jnp.int32, shape, 0)
    ys = y + yz * SIDE
    z = lax.broadcasted_iota(jnp.int32, shape, 1)
    keep = (ys > 0) & (ys < last_y) & (z > 0) & (z < DEPTH - 1)
    for x in range(SIDE):
        inside = keep & (gx * SIDE + x > 0) & (gx * SIDE + x < last_x)
        scale = None
        for c in range(4):
            value = grid[c, x + 1, 1 : SIDE + 1, :]
            if x == 0:
                value = value + xlow[c, 1 : SIDE + 1, :]
            if x == SIDE - 1:
                value = value + xhigh[c, 1 : SIDE + 1, :]
            value = value + jnp.where(y == 0, ylow[c, x : x + 1, :], 0.0)
            value = value + jnp.where(y == SIDE - 1, yhigh[c, x : x + 1, :], 0.0)
            if c == 0:
                mass[x] = value
                scale = 1.0 / jnp.maximum(value, 0.5)
            else:
                value = value * scale
                if c == 3:
                    value = value - 0.5
                speed[c - 1, x] = jnp.where(inside, value, 0.0)


def passed_along(array, axis, by):
    devices = lax.axis_size(axis)
    pairs = [(i, i + by) for i in range(devices) if 0 <= i + by < devices]
    return lax.ppermute(array, axis, pairs)


VMEM = pl.BlockSpec(memory_space=pltpu.VMEM)
HBM = pl.BlockSpec(memory_space=pltpu.HBM)
SMEM = pl.BlockSpec(memory_space=pltpu.SMEM)
PARAMS = pltpu.CompilerParams(vmem_limit_bytes=40 * 1024 * 1024)


def local(owners, bricks, cells, offsets, mass, velocity, affine):
    nblk, lanes = mass.shape
    ndev = lax.axis_size("gx") * lax.axis_size("yz")
    cap = 2 * nblk // ndev
    parts = min(PARTS, cap)
    part = cap // parts
    packed = pl.pallas_call(
        functools.partial(pack_kernel, parts=parts),
        out_shape=[jax.ShapeDtypeStruct((ndev, NCH, part, lanes), jnp.float32)] * parts,
        in_specs=[SMEM, SMEM] + [HBM] * 5,
        out_specs=[VMEM] * parts,
        scratch_shapes=[
            pltpu.VMEM((3, nblk, lanes), jnp.int32),
            pltpu.VMEM((3, nblk, lanes), jnp.float32),
            pltpu.VMEM((nblk, lanes), jnp.float32),
            pltpu.VMEM((3, nblk, lanes), jnp.float32),
            pltpu.VMEM((9, nblk, lanes), jnp.float32),
            pltpu.SMEM((ndev,), jnp.int32),
            pltpu.SMEM((parts * nblk,), jnp.int32),
            pltpu.SMEM((parts,), jnp.int32),
            pltpu.SemaphoreType.DMA((5,)),
        ],
        name="pack",
    )(
        owners[:, 0],
        bricks,
        jnp.transpose(cells, (1, 0, 2)),
        jnp.transpose(offsets, (1, 0, 2)),
        mass,
        jnp.transpose(velocity, (1, 0, 2)),
        jnp.transpose(affine, (1, 0, 2)),
    )
    moved = []
    for p in packed:
        if moved:
            p, moved[-1] = lax.optimization_barrier((p, moved[-1]))
        moved.append(lax.all_to_all(p, ("gx", "yz"), split_axis=0, concat_axis=0, tiled=True))
    sums = []
    for arrived in moved:
        codes = arrived[:, NCH - 1, :, 0].astype(jnp.int32).reshape(ndev * part)
        sums = [
            pl.pallas_call(
                functools.partial(tile_kernel, not sums),
                out_shape=jax.ShapeDtypeStruct((DEPTH // 8, NUV, 64, DEPTH), jnp.float32),
                in_specs=[SMEM, VMEM] + [VMEM] * len(sums),
                out_specs=VMEM,
                scratch_shapes=[pltpu.SMEM((ndev * part + 1,), jnp.int32)],
                compiler_params=PARAMS,
                cost_estimate=pl.CostEstimate(
                    flops=40_000_000_000 // parts, bytes_accessed=4_000_000, transcendentals=0
                ),
                name="tiles",
            )(codes, arrived, *sums)
        ]
    grid = pl.pallas_call(
        place_kernel,
        out_shape=jax.ShapeDtypeStruct((4, SIDE + 2, SIDE + 2, DEPTH), jnp.float32),
        in_specs=[VMEM],
        out_specs=VMEM,
        scratch_shapes=[
            pltpu.VMEM((2 * NUV * 64, (DEPTH // 8) * DEPTH), jnp.bfloat16),
            pltpu.VMEM(((DEPTH // 8) * DEPTH, DEPTH), jnp.int32),
        ],
        compiler_params=PARAMS,
        name="place",
    )(*sums)
    xlow = passed_along(grid[:, SIDE + 1], "gx", 1)
    xhigh = passed_along(grid[:, 0], "gx", -1)

    def y_face(at):
        face = grid[:, 1 : SIDE + 1, at]
        face = face.at[:, 0].add(xlow[:, at])
        return face.at[:, SIDE - 1].add(xhigh[:, at])

    ylow = passed_along(y_face(SIDE + 1), "yz", 1)
    yhigh = passed_along(y_face(0), "yz", -1)
    return pl.pallas_call(
        finish_kernel,
        out_shape=(
            jax.ShapeDtypeStruct((SIDE, SIDE, DEPTH), jnp.float32),
            jax.ShapeDtypeStruct((3, SIDE, SIDE, DEPTH), jnp.float32),
        ),
        in_specs=[VMEM] * 5,
        out_specs=(VMEM, VMEM),
        compiler_params=PARAMS,
        name="finish",
    )(grid, xlow, xhigh, ylow, yhigh)


def solution(mesh):
    block = ("gx", "yz")
    return jax.shard_map(
        local,
        mesh=mesh,
        in_specs=(
            P(block, None),
            P(block),
            P(block, None, None),
            P(block, None, None),
            P(block, None),
            P(block, None, None),
            P(block, None, None),
        ),
        out_specs=(P("gx", "yz", None), P(None, "gx", "yz", None)),
        check_vma=False,
    )
```

```python
import functools

import jax
import jax.numpy as jnp
from jax import lax
from jax.experimental import pallas as pl
from jax.experimental.pallas import tpu as pltpu
from jax.sharding import PartitionSpec as P

SIDE = 16
DEPTH = 128
ROWS = 104
NCH = 17
NUV = 4
PARTS = 2
GROUP = 8


def pack_kernel(owners, bricks, *rest, parts):
    sources, outs = rest[:5], rest[5 : 5 + parts]
    held, (count, listed, slots, sems) = rest[5 + parts : 10 + parts], rest[10 + parts :]
    copies = [pltpu.make_async_copy(s, h, sems.at[i]) for i, (s, h) in enumerate(zip(sources, held))]
    for copy in copies:
        copy.start()
    cells, offsets, mass, velocity, affine = held
    nblk = mass.shape[0]
    ndev, _, part, lanes = outs[0].shape
    for out in outs:
        out[:, NCH - 1] = jnp.full((ndev, part, lanes), -1.0, jnp.float32)

    def clear(i, carry):
        count[i] = 0
        return carry

    lax.fori_loop(0, ndev, clear, 0)

    for i in range(parts):
        slots[i] = 0

    def rank(g, carry):
        d = owners[g]
        k = count[d]
        count[d] = k + 1
        mine = lax.div(k, part)
        n = slots[mine]
        slots[mine] = n + 1
        listed[mine * nblk + n] = (d * part + (k - mine * part)) * nblk + g
        return carry

    lax.fori_loop(0, nblk, rank, 0)
    for copy in copies:
        copy.wait()
    for i, out in enumerate(outs):
        size = slots[i]

        def move(n, i=i, out=out):
            item = listed[i * nblk + n]
            at = lax.div(item, nblk)
            g = item - at * nblk
            d = lax.div(at, part)
            slot = pl.ds(at - d * part, 1)
            row = pl.ds(g, 1)
            for j in range(3):
                out[d, j, slot, :] = offsets[j, row, :]
                out[d, 4 + j, slot, :] = velocity[j, row, :]
            out[d, 3, slot, :] = mass[row, :]
            for j in range(9):
                out[d, 7 + j, slot, :] = affine[j, row, :]
            flat = cells[0, row, :] * 64 + cells[1, row, :] * 8 + cells[2, row, :]
            out[d, NCH - 1, slot, :] = (flat + bricks[g] * 512).astype(jnp.float32)

        def moves(n, carry, size=size, move=move):
            move(2 * n)
            move(jnp.minimum(2 * n + 1, size - 1))
            return carry

        lax.fori_loop(0, lax.div(size + 1, 2), moves, 0)


def halves(values):
    high = values.astype(jnp.bfloat16)
    low = (values - high.astype(jnp.float32)).astype(jnp.bfloat16)
    return high, low


def weights(place, frac):
    first = 0.5 * (1.5 - frac) ** 2
    middle = 0.75 - (frac - 1.0) ** 2
    last = 0.5 * (frac - 0.5) ** 2
    spread = jnp.where(place == 2.0, last, 0.0)
    spread = jnp.where(place == 1.0, middle, spread)
    return jnp.where(place == 0.0, first, spread)


def tile_kernel(first, codes, moved, *rest):
    acc, chosen = rest[-2:]
    ndev, _, part, lanes = moved.shape
    slots = ndev * part

    def choose(s, n):
        chosen[n] = s
        return n + jnp.where(codes[s] >= 0, 1, 0)

    total = lax.fori_loop(0, slots, choose, 0)
    if first:
        acc[...] = jnp.zeros_like(acc)
    else:
        acc[...] = rest[0][...]
    row = lax.broadcasted_iota(jnp.int32, (ROWS, lanes), 0)
    row_x = (row // 10).astype(jnp.float32)
    row_z = (row % 10).astype(jnp.float32)
    row_y = lax.broadcasted_iota(jnp.int32, (16, lanes), 0).astype(jnp.float32)
    none = jnp.zeros((16, lanes), jnp.float32)
    fill = jnp.zeros((lanes - ROWS, 3 * lanes), jnp.float32)

    def block(n):
        s = chosen[n]
        d = lax.div(s, part)
        slot = pl.ds(s - d * part, 1)
        brick = codes[s] >> 9
        uv = lax.div(brick, DEPTH // 8)
        w = lax.rem(brick, DEPTH // 8)
        ch = lambda j: moved[d, j, slot, :]
        flat = ch(NCH - 1).astype(jnp.int32) & 511
        cell_x = (flat >> 6).astype(jnp.float32)
        cell_y = ((flat >> 3) & 7).astype(jnp.float32)
        cell_z = (flat & 7).astype(jnp.float32)
        fx, fy, fz = ch(0), ch(1), ch(2)
        m = ch(3)
        ex = row_x - cell_x
        ey = row_y - cell_y
        ez = row_z - cell_z
        ry = ey - fy
        wy = weights(ey, fy)
        wxz = weights(ex, fx) * weights(ez, fz)
        big = jnp.concatenate([wxz, wxz * (ex - fx), wxz * (ez - fz)], 1)
        small = [jnp.concatenate([wy * m, none, none], 1)]
        for i in range(3):
            plain = wy * (m * ch(4 + i) + ch(8 + 3 * i) * ry)
            small.append(jnp.concatenate([plain, wy * ch(7 + 3 * i), wy * ch(9 + 3 * i)], 1))
        sh, sl = halves(jnp.concatenate(small, 0))
        bh, bl = halves(jnp.concatenate([big, fill], 0))
        both = lax.dot_general(
            jnp.concatenate([sh, sl], 0),
            jnp.concatenate([bh, bl], 0),
            (((1,), (1,)), ((), ())),
            preferred_element_type=jnp.float32,
        )
        return w, uv, both[:64, :lanes] + (both[:64, lanes:] + both[64:, :lanes])

    def add_blocks(n, carry, group):
        for w, uv, tile in [block(n + i) for i in range(group)]:
            acc[w, uv] += tile
        return carry

    paired = total // GROUP * GROUP
    lax.fori_loop(0, total // GROUP, lambda n, c: add_blocks(n * GROUP, c, GROUP), 0)
    lax.fori_loop(paired, total, lambda n, c: add_blocks(n, c, 1), 0)


def place_kernel(acc, grid, wide, key):
    depth_bricks = DEPTH // 8
    rows = NUV * 64
    for w in range(depth_bricks):
        high, low = halves(acc[w].reshape(rows, DEPTH))
        wide[:rows, w * DEPTH : (w + 1) * DEPTH] = high
        wide[rows:, w * DEPTH : (w + 1) * DEPTH] = low
    k = lax.broadcasted_iota(jnp.int32, key.shape, 0)
    spot = k & (DEPTH - 1)
    x = spot // 10
    key[...] = x * 1024 + (spot - x * 10) + (k // DEPTH) * 8 - 1
    lane = lax.broadcasted_iota(jnp.int32, key.shape, 1)
    grid[...] = jnp.zeros_like(grid)
    for pair in range(5):
        pick = jnp.concatenate(
            [
                jnp.where(key[...] == lane + (2 * pair + i) * 1024, 1.0, 0.0).astype(jnp.bfloat16)
                for i in range(2)
            ],
            1,
        )
        put = jnp.dot(wide[...], pick, preferred_element_type=jnp.float32)
        put = put[:rows] + put[rows:]
        for i in range(2):
            x = 2 * pair + i
            for uv in range(NUV):
                u, v = uv // 2, uv % 2
                for c in range(4):
                    base = uv * 64 + c * 16
                    grid[c, 8 * u + x, 8 * v : 8 * v + 10, :] += put[
                        base : base + 10, i * DEPTH : (i + 1) * DEPTH
                    ]


def last_kernel(first, codes, moved, *rest):
    grid, acc, chosen, wide, key = rest[-5:]
    tile_kernel(first, codes, moved, *rest[:-5], acc, chosen)
    place_kernel(acc, grid, wide, key)


def finish_kernel(grid, xlow, xhigh, ylow, yhigh, mass, speed):
    gx, yz = lax.axis_index("gx"), lax.axis_index("yz")
    last_x = SIDE * lax.axis_size("gx") - 1
    last_y = SIDE * lax.axis_size("yz") - 1
    shape = (SIDE, DEPTH)
    y = lax.broadcasted_iota(jnp.int32, shape, 0)
    ys = y + yz * SIDE
    z = lax.broadcasted_iota(jnp.int32, shape, 1)
    keep = (ys > 0) & (ys < last_y) & (z > 0) & (z < DEPTH - 1)
    for x in range(SIDE):
        inside = keep & (gx * SIDE + x > 0) & (gx * SIDE + x < last_x)
        scale = None
        for c in range(4):
            value = grid[c, x + 1, 1 : SIDE + 1, :]
            if x == 0:
                value = value + xlow[c, 1 : SIDE + 1, :]
            if x == SIDE - 1:
                value = value + xhigh[c, 1 : SIDE + 1, :]
            value = value + jnp.where(y == 0, ylow[c, x : x + 1, :], 0.0)
            value = value + jnp.where(y == SIDE - 1, yhigh[c, x : x + 1, :], 0.0)
            if c == 0:
                mass[x] = value
                scale = 1.0 / jnp.maximum(value, 0.5)
            else:
                value = value * scale
                if c == 3:
                    value = value - 0.5
                speed[c - 1, x] = jnp.where(inside, value, 0.0)


def passed_along(array, axis, by):
    devices = lax.axis_size(axis)
    pairs = [(i, i + by) for i in range(devices) if 0 <= i + by < devices]
    return lax.ppermute(array, axis, pairs)


VMEM = pl.BlockSpec(memory_space=pltpu.VMEM)
HBM = pl.BlockSpec(memory_space=pltpu.HBM)
SMEM = pl.BlockSpec(memory_space=pltpu.SMEM)
PARAMS = pltpu.CompilerParams(vmem_limit_bytes=40 * 1024 * 1024)


def local(owners, bricks, cells, offsets, mass, velocity, affine):
    nblk, lanes = mass.shape
    ndev = lax.axis_size("gx") * lax.axis_size("yz")
    cap = 2 * nblk // ndev
    parts = min(PARTS, cap)
    part = cap // parts
    packed = pl.pallas_call(
        functools.partial(pack_kernel, parts=parts),
        out_shape=[jax.ShapeDtypeStruct((ndev, NCH, part, lanes), jnp.float32)] * parts,
        in_specs=[SMEM, SMEM] + [HBM] * 5,
        out_specs=[VMEM] * parts,
        scratch_shapes=[
            pltpu.VMEM((3, nblk, lanes), jnp.int32),
            pltpu.VMEM((3, nblk, lanes), jnp.float32),
            pltpu.VMEM((nblk, lanes), jnp.float32),
            pltpu.VMEM((3, nblk, lanes), jnp.float32),
            pltpu.VMEM((9, nblk, lanes), jnp.float32),
            pltpu.SMEM((ndev,), jnp.int32),
            pltpu.SMEM((parts * nblk,), jnp.int32),
            pltpu.SMEM((parts,), jnp.int32),
            pltpu.SemaphoreType.DMA((5,)),
        ],
        name="pack",
    )(
        owners[:, 0],
        bricks,
        jnp.transpose(cells, (1, 0, 2)),
        jnp.transpose(offsets, (1, 0, 2)),
        mass,
        jnp.transpose(velocity, (1, 0, 2)),
        jnp.transpose(affine, (1, 0, 2)),
    )
    moved = []
    for p in packed:
        if moved:
            p, moved[-1] = lax.optimization_barrier((p, moved[-1]))
        moved.append(lax.all_to_all(p, ("gx", "yz"), split_axis=0, concat_axis=0, tiled=True))
    held = (DEPTH // 8, NUV, 64, DEPTH)
    sums = []
    for i, arrived in enumerate(moved):
        codes = arrived[:, NCH - 1, :, 0].astype(jnp.int32).reshape(ndev * part)
        last = i == parts - 1
        chosen = pltpu.SMEM((ndev * part + 1,), jnp.int32)
        scratch = [
            pltpu.VMEM(held, jnp.float32),
            chosen,
            pltpu.VMEM((2 * NUV * 64, (DEPTH // 8) * DEPTH), jnp.bfloat16),
            pltpu.VMEM(((DEPTH // 8) * DEPTH, DEPTH), jnp.int32),
        ]
        shape = (4, SIDE + 2, SIDE + 2, DEPTH) if last else held
        sums = [
            pl.pallas_call(
                functools.partial(last_kernel if last else tile_kernel, not sums),
                out_shape=jax.ShapeDtypeStruct(shape, jnp.float32),
                in_specs=[SMEM, VMEM] + [VMEM] * len(sums),
                out_specs=VMEM,
                scratch_shapes=scratch if last else [chosen],
                compiler_params=PARAMS,
                cost_estimate=pl.CostEstimate(
                    flops=40_000_000_000 // parts, bytes_accessed=4_000_000, transcendentals=0
                ),
                name="last_tiles" if last else "tiles",
            )(codes, arrived, *sums)
        ]
    grid = sums[0]
    xlow = passed_along(grid[:, SIDE + 1], "gx", 1)
    xhigh = passed_along(grid[:, 0], "gx", -1)

    def y_face(at):
        face = grid[:, 1 : SIDE + 1, at]
        face = face.at[:, 0].add(xlow[:, at])
        return face.at[:, SIDE - 1].add(xhigh[:, at])

    ylow = passed_along(y_face(SIDE + 1), "yz", 1)
    yhigh = passed_along(y_face(0), "yz", -1)
    return pl.pallas_call(
        finish_kernel,
        out_shape=(
            jax.ShapeDtypeStruct((SIDE, SIDE, DEPTH), jnp.float32),
            jax.ShapeDtypeStruct((3, SIDE, SIDE, DEPTH), jnp.float32),
        ),
        in_specs=[VMEM] * 5,
        out_specs=(VMEM, VMEM),
        compiler_params=PARAMS,
        name="finish",
    )(grid, xlow, xhigh, ylow, yhigh)


def solution(mesh):
    block = ("gx", "yz")
    return jax.shard_map(
        local,
        mesh=mesh,
        in_specs=(
            P(block, None),
            P(block),
            P(block, None, None),
            P(block, None, None),
            P(block, None),
            P(block, None, None),
            P(block, None, None),
        ),
        out_specs=(P("gx", "yz", None), P(None, "gx", "yz", None)),
        check_vma=False,
    )
```
